256 devices in a mesh: occ: 8 (over x_hi, y), vir: 32 (over x_lo, z, core).
Axes of the slice: x: 4 (x_hi: 2, x_lo: 2; x = x_hi * 2 + x_lo), y: 4, z: 8, core: 2. Of those that a mesh axis runs over, the one named last changes fastest.
Arguments:
- t2: float32 [512, 24576], P('occ', 'vir'), may hold values from -6 to 6
- integral_tiles: float32 [8, 2048, 128, 128], P('occ', 'vir'), may hold values from -0.0546875 to 0.0546875
- contract_tile: int32 [8, 2048], P('occ', 'vir'), may hold values from 0 to 5
- slot_of_block: int32 [8, 2048], P('occ', 'vir'), may hold values from 0 to 31
- residual_list: int32 [32, 32], replicated, may hold values from 0 to 191, as said below
- owner_pos: int32 [192], replicated, may hold values from 0 to 191, as said below
Outputs:
- ladder_residual: float32 [512, 24576], P('occ', 'vir')
The draws below stay inside these ranges and needn't reach their ends.
Inputs may be any that keep to these rules, and one draw needn't show every extreme that they name: `residual_list`: each row names 32 distinct tiles; their owners owner_pos // 6 are 16 distinct values, each owning exactly 2 of the row's tiles. `owner_pos`: A permutation of the 192 tiles.
All inputs are finite; a program needn't handle non-finite values.
Results may differ from the reference program's by a relative error of at most 0.0001.
Values sent between devices are 32-bit elements; how exact they have to be, the bound alone decides.
No kernel may reach another device: no remote copies, remote signals or barrier semaphores. Data moves between devices by JAX's collectives and lax.ppermute only.
A program may use at most 128 MiB of HBM per device.

```python
import jax
import jax.numpy as jnp
from jax import lax

TILE = 128
TILES_DEV = 6
CAP = 2
NZ_DEV = 64
NIJ = 512
NT = 192
SLOTS = 32
N_OCC = 8
N_VIR = 32


def route_tables(key):
    position = jax.random.permutation(jax.random.fold_in(key, 11), NT).astype(jnp.int32)
    inverse = jnp.argsort(position).astype(jnp.int32)
    group_keys = jax.random.split(jax.random.fold_in(key, 12), N_VIR)

    def one_list(group_key):
        owner_key, local_key = jax.random.split(group_key)
        owners = jax.random.permutation(owner_key, N_VIR)[:SLOTS // 2].astype(jnp.int32)
        local_keys = jax.random.split(local_key, SLOTS // 2)
        chosen = jax.vmap(lambda k: jax.random.permutation(k, TILES_DEV)[:CAP])(local_keys).astype(jnp.int32)
        places = (owners[:, None] * TILES_DEV + chosen).reshape(-1)
        return inverse[places]
    lists = jax.vmap(one_list)(group_keys).astype(jnp.int32)
    return (lists, position)


def draw_residual_list(key, part):
    lists, position = route_tables(key)
    return lists


def draw_owner_pos(key, part):
    lists, position = route_tables(key)
    return position


def set_ends(values, key, least, top_value):
    index_at = [jax.random.randint(jax.random.fold_in(key, axis), (), 0, length) for axis, length in enumerate(values.shape)]
    widest = values.shape.index(max(values.shape))
    next_to = index_at[:widest] + [(index_at[widest] + 1) % values.shape[widest]] + index_at[widest + 1:]
    return values.at[tuple(index_at)].set(least).at[tuple(next_to)].set(top_value)


def level_of(stream_key, dims, shards, least, largest):
    def one(dim, parts):
        steps = jax.random.uniform(jax.random.fold_in(jax.random.fold_in(stream_key, 6), dim), (parts,), jnp.float32, least / len(shards), largest / len(shards))
        return jnp.repeat(jnp.exp(steps), dims[dim] // parts).reshape((-1,) + (1,) * (len(dims) - dim - 1))

    gain = one(*shards[0])
    for cut in shards[1:]:
        gain = gain * one(*cut)
    return gain


def scatter_about(stream_key, shape, deviation, limit, cuts=(), kind=jnp.bfloat16):
    values = jax.random.normal(stream_key, shape, jnp.float32) * deviation
    if len(cuts) > 0:
        values = level_of(stream_key, shape, cuts, -0.22, 0.18) * values
    return jnp.clip(values, min=-limit, max=limit).astype(kind)


def setup_inputs(seed: int = 0) -> dict:
    key_of = jax.random.split(jax.random.key(seed), 7)
    t2 = scatter_about(key_of[0], (NIJ, NT * TILE), 1.0, 6.0, ((0, 8), (1, 32)), jnp.float32)
    integral_tiles = scatter_about(key_of[1], (N_OCC, N_VIR * NZ_DEV, TILE, TILE), (TILE * N_OCC * NZ_DEV // TILES_DEV) ** -0.5, 0.0546875, ((0, 8), (1, 32)), jnp.float32)
    contract_tile = set_ends(jax.random.randint(key_of[2], (N_OCC, N_VIR * NZ_DEV), 0, TILES_DEV), jax.random.fold_in(key_of[2], 1), 0, TILES_DEV - 1).astype(jnp.int32)
    slot_of_block = set_ends(jax.random.randint(key_of[3], (N_OCC, N_VIR * NZ_DEV), 0, SLOTS), jax.random.fold_in(key_of[3], 1), 0, SLOTS - 1).astype(jnp.int32)
    residual_list = draw_residual_list(jax.random.fold_in(key_of[6], 71), 0)
    owner_pos = draw_owner_pos(jax.random.fold_in(key_of[6], 71), 0)
    return {"t2": t2, "integral_tiles": integral_tiles, "contract_tile": contract_tile, "slot_of_block": slot_of_block, "residual_list": residual_list, "owner_pos": owner_pos}


def reference(t2, integral_tiles, contract_tile, slot_of_block, residual_list, owner_pos):
    start_total = jnp.zeros((NIJ, NT, TILE), jnp.float32)

    def vir_group(vir_idx, total):
        vir_idx = vir_idx.astype(jnp.int32)
        first = (vir_idx * NZ_DEV).astype(jnp.int32)
        blocks = lax.dynamic_slice_in_dim(integral_tiles, first, NZ_DEV, 1).reshape(N_OCC * NZ_DEV, TILE, TILE)
        rows_c = lax.dynamic_slice_in_dim(contract_tile, first, NZ_DEV, 1).reshape(-1)
        rows_s = lax.dynamic_slice_in_dim(slot_of_block, first, NZ_DEV, 1).reshape(-1)
        dense_map = jnp.zeros((TILES_DEV, TILE, SLOTS, TILE), jnp.float32)
        dense_map = dense_map.at[rows_c, :, rows_s, :].add(blocks)
        dense_map = dense_map.reshape(TILES_DEV * TILE, SLOTS * TILE)
        column_start = (vir_idx * TILES_DEV * TILE).astype(jnp.int32)
        columns = lax.dynamic_slice_in_dim(t2, column_start, TILES_DEV * TILE, 1)
        partial_value = jnp.dot(columns, dense_map, precision=lax.Precision.HIGHEST, preferred_element_type=jnp.float32)
        targets = owner_pos[residual_list[vir_idx]]
        return total.at[:, targets, :].add(partial_value.reshape(NIJ, SLOTS, TILE))

    total = lax.fori_loop(0, N_VIR, vir_group, start_total)
    return total.reshape(NIJ, NT * TILE)
```

```python
import functools

import jax
import jax.numpy as jnp
from jax import lax
from jax.experimental import pallas as pl
from jax.experimental.pallas import tpu as pltpu
from jax.sharding import PartitionSpec as P

N_Y = 4
N_XH = 2
N_Z = 8
N_XL = 2
ROWS_A = 40
PRODUCT_MIB = 62


def from_occ(v, dx, dy):
    perm = [
        (((a + dx) % N_XH) * N_Y + (b + dy) % N_Y, a * N_Y + b)
        for a in range(N_XH)
        for b in range(N_Y)
    ]
    return lax.ppermute(v, "occ", perm)


def from_vir(v, dx, dc):
    perm = [
        ((((a + dx) % N_XL) * N_Z + z) * 2 + (c + dc) % 2, (a * N_Z + z) * 2 + c)
        for a in range(N_XL)
        for z in range(N_Z)
        for c in range(2)
    ]
    return lax.ppermute(v, "vir", perm)


def smem():
    return pl.BlockSpec(memory_space=pltpu.SMEM)


def vmem():
    return pl.BlockSpec(memory_space=pltpu.VMEM)


def hbm():
    return pl.BlockSpec(memory_space=pltpu.HBM)


def call(kernel, out_shape, in_specs, out_specs, scratch, nbytes, flops=0, limit=8):
    return pl.pallas_call(
        kernel,
        out_shape=out_shape,
        in_specs=in_specs,
        out_specs=out_specs,
        scratch_shapes=scratch,
        compiler_params=pltpu.CompilerParams(vmem_limit_bytes=limit * 1024 * 1024),
        cost_estimate=pl.CostEstimate(flops=flops, bytes_accessed=nbytes, transcendentals=0),
    )


def product_kernel(n_pieces, moves, *refs):
    con_ref, slot_ref, blocks = refs[:3]
    pieces = refs[3 : 3 + n_pieces]
    b_ref, t_ref, x_ref, acc_ref, block_sems, in_sems, out_sems = refs[-7:]
    outs = refs[3 + n_pieces : -7]
    n_blocks, width, _ = b_ref.shape
    n_parts = block_sems.shape[0]
    part = n_blocks // n_parts
    tiles = x_ref.shape[0]
    loads = []
    rows = pieces[0].shape[0]
    for i, piece in enumerate(pieces):
        load = pltpu.make_async_copy(piece, t_ref.at[pl.ds(i * rows, rows)], in_sems.at[i])
        load.start()
        loads.append(load)
    block_loads = []
    for i in range(n_parts):
        some = pl.ds(i * part, part)
        load = pltpu.make_async_copy(blocks.at[some], b_ref.at[some], block_sems.at[i])
        load.start()
        block_loads.append(load)
    acc_ref[...] = jnp.zeros_like(acc_ref)
    for i, load in enumerate(loads):
        load.wait()
        here = slice(i * rows, (i + 1) * rows)
        for c in range(tiles):
            a = t_ref[here, c * width : (c + 1) * width]
            high = a.astype(jnp.bfloat16)
            x_ref[c, here, :width] = high
            x_ref[c, here, width:] = (a - high.astype(jnp.float32)).astype(jnp.bfloat16)
    step = 4

    def body(k, carry):
        results = []
        for u in range(step):
            b = b_ref[k * step + u]
            high = b.astype(jnp.bfloat16)
            low = (b - high.astype(jnp.float32)).astype(jnp.bfloat16)
            w = jnp.concatenate([high, low], axis=1)
            w = jnp.concatenate([w, w], axis=0)
            x = x_ref[con_ref[0, k * step + u]]
            p = jnp.dot(x, w, preferred_element_type=jnp.float32)
            results.append(p[:, :width] + p[:, width:])
        for u in range(step):
            s = slot_ref[0, k * step + u]
            acc_ref[s] = acc_ref[s] + results[u]
        return carry

    for i, load in enumerate(block_loads):
        load.wait()
        lax.fori_loop(i * part // step, (i + 1) * part // step, body, 0)
    stores = []
    for n, (o, index, slot, slots, row, n_rows) in enumerate(moves):
        source = acc_ref.at[pl.ds(slot, slots), pl.ds(row, n_rows)]
        target = outs[o] if index is None else outs[o].at[index]
        store = pltpu.make_async_copy(source, target, out_sems.at[n])
        store.start()
        stores.append(store)
    for store in stores:
        store.wait()


def products(con, slot, blocks, pieces, slots, shapes, moves):
    n_blocks, width, _ = blocks.shape
    tiles = pieces[0].shape[1] // width
    n_rows = pieces[0].shape[0] * len(pieces)
    shapes = [jax.ShapeDtypeStruct(s, jnp.float32) for s in shapes]
    return call(
        functools.partial(product_kernel, len(pieces), moves),
        shapes,
        [smem(), smem()] + [hbm()] * (1 + len(pieces)),
        [hbm()] * len(shapes),
        [
            pltpu.VMEM(blocks.shape, jnp.float32),
            pltpu.VMEM((n_rows, tiles * width), jnp.float32),
            pltpu.VMEM((tiles, n_rows, 2 * width), jnp.bfloat16),
            pltpu.VMEM((slots, n_rows, width), jnp.float32),
            pltpu.SemaphoreType.DMA((4,)),
            pltpu.SemaphoreType.DMA((len(pieces),)),
            pltpu.SemaphoreType.DMA((len(moves),)),
        ],
        4 * (blocks.size + n_rows * (tiles + slots) * width),
        8 * n_blocks * n_rows * width * width,
        PRODUCT_MIB,
    )(con, slot, blocks, *pieces)


def sum_kernel(own, left_a, left_b, right_a, right_b, keep, give):
    half = left_a.shape[1]
    for out, d in ((give, 1), (keep, 0)):
        out[:half] = own[d, :half] + left_a[d] + right_a[d]
        out[half:] = own[d, half:] + left_b[d] + right_b[d]


def y_sum(own, left_a, left_b, right_a, right_b):
    shape = jax.ShapeDtypeStruct(own.shape[1:], jnp.float32)
    return call(sum_kernel, [shape] * 2, [vmem()] * 5, [vmem()] * 2, [], 16 * own.size)(
        own, left_a, left_b, right_a, right_b
    )


def pad_kernel(table, keep, other_a, own, other_b, left_a, left_b, right_a, right_b, out, total):
    half = left_a.shape[0]
    rows_a = keep.shape[1]
    total[:, :rows_a] = keep[...] + other_a[...]
    lower, upper = slice(0, half), slice(half, None)
    for part, left, right in ((lower, left_a, right_a), (upper, left_b, right_b)):
        total[part, rows_a:] = (own[part] + other_b[3, part]) + (left[...] + right[...])

    def body(k, carry):
        s = table[k]

        @pl.when(s >= 0)
        def _():
            out[k] = total[s]

        @pl.when(s < 0)
        def _():
            out[k] = jnp.zeros_like(out[k])

        return carry

    lax.fori_loop(0, out.shape[0], body, 0)


def pad(table, *terms):
    slots, rows_a, width = terms[0].shape
    rows = rows_a + terms[2].shape[1]
    shape = jax.ShapeDtypeStruct((table.shape[0], rows, width), jnp.float32)
    scratch = [pltpu.VMEM((slots, rows, width), jnp.float32)]
    return call(
        pad_kernel, shape, [smem()] + [vmem()] * 8, vmem(), scratch, 24 * slots * rows * width
    )(table, *terms)


def to_owners(padded, groups):
    n, rows, width = padded.shape
    pieces = lax.all_to_all(padded.reshape(groups, n // groups, rows, width), "vir", 0, 0)
    return pieces.reshape(n, rows, width)


def finish_kernel(place, pieces, out, acc):
    acc[...] = jnp.zeros_like(acc)

    def body(k, carry):
        p = place[k]

        @pl.when(p >= 0)
        def _():
            acc[p] = acc[p] + pieces[k]

        return carry

    lax.fori_loop(0, pieces.shape[0], body, 0)
    tiles, _, width = acc.shape
    for c in range(tiles):
        out[:, c * width : (c + 1) * width] = acc[c]


def finish(place, pieces, tiles):
    _, rows, width = pieces.shape
    shape = jax.ShapeDtypeStruct((rows, tiles * width), jnp.float32)
    scratch = [pltpu.VMEM((tiles, rows, width), jnp.float32)]
    return call(finish_kernel, shape, [smem(), vmem()], vmem(), scratch, 4 * pieces.size)(
        place, pieces
    )


def routes(residual_list, owner_pos, tiles_dev, me):
    groups, slots = residual_list.shape
    total = owner_pos.shape[0]
    tiles = jnp.arange(total, dtype=jnp.int32)
    positions = jnp.sum(
        jnp.where(residual_list[:, :, None] == tiles, owner_pos, 0), axis=2, dtype=jnp.int32
    )
    owners = jnp.arange(groups, dtype=jnp.int32)
    index = jnp.arange(slots, dtype=jnp.int32)
    before = index[None, :] < index[:, None]

    def row(v):
        return jnp.sum(jnp.where(owners[:, None] == v, positions, 0), axis=0, dtype=jnp.int32)

    def pick(mask, value):
        rank = jnp.sum(mask[:, None, :] & before, axis=2, dtype=jnp.int32)
        chosen = mask[:, :, None] & (rank[:, :, None] == jnp.arange(2, dtype=jnp.int32))
        return jnp.max(jnp.where(chosen, value[:, :, None], -1), axis=1).reshape(-1)

    own = row(me)
    to_owner = (own // tiles_dev)[None, :] == owners[:, None]
    send = pick(to_owner, jnp.broadcast_to(index, (groups, slots)))
    place = pick(positions // tiles_dev == me, positions % tiles_dev)
    return send, place


def shards(t2, integral_tiles, contract_tile, slot_of_block, residual_list, owner_pos):
    width = integral_tiles.shape[-1]
    tiles_dev = t2.shape[1] // width
    groups, slots = residual_list.shape
    half = slots // 2
    rows_a = ROWS_A
    rows = t2.shape[0]
    rows_b = rows - rows_a

    me = lax.axis_index("vir")
    send, place = routes(residual_list, owner_pos, tiles_dev, me)
    offsets = [(dx, dy) for dy in (2, 1, -1, 0) for dx in (0, 1)]
    pieces = [from_occ(t2, dx, dy) if dx or dy else t2 for dx, dy in offsets]

    one = (slots, rows_b, width)
    shapes = [(2, half, rows_a, width)] * 6 + [(2, slots, rows_a, width)] + [one] * 4 + [(4,) + one]
    moves = []
    for g in range(4):
        for part in range(2) if g < 3 else (None,):
            for d in range(2):
                row = (2 * g + d) * rows
                if part is None:
                    moves.append((6, d, 0, slots, row, rows_a))
                else:
                    moves.append((2 * g + part, d, part * half, half, row, rows_a))
        moves.append((7 + g, None, 0, slots, 2 * g * rows + rows_a, rows_b))
        moves.append((11, g, 0, slots, (2 * g + 1) * rows + rows_a, rows_b))
    far_a, far_b, up_a, up_b, down_a, down_b, own, far, up, down, here, give_b = products(
        contract_tile, slot_of_block, integral_tiles[0], pieces, slots, shapes, moves
    )
    other_b = from_occ(give_b, 1, 0)
    left_far = from_occ(far_a, 0, -1)
    right_far = from_occ(far_b, 0, 1)
    left_b = from_occ(up_b, 0, -1)
    right_a = from_occ(down_a, 0, 1)
    left_a = from_occ(up_a + left_far, 0, -1)
    right_b = from_occ(down_b + right_far, 0, 1)
    sums_a = (own, left_a, left_b, right_a, right_b)

    left_far = from_occ(far[:half] + other_b[0, :half], 0, -1)
    right_far = from_occ(far[half:] + other_b[0, half:], 0, 1)
    left_b = from_occ(up[half:] + other_b[1, half:], 0, -1)
    right_a = from_occ(down[:half] + other_b[2, :half], 0, 1)
    left_a = from_occ(up[:half] + other_b[1, :half] + left_far, 0, -1)
    right_b = from_occ(down[half:] + other_b[2, half:] + right_far, 0, 1)

    keep, give = y_sum(*sums_a)
    other = from_occ(give, 1, 0)
    padded = pad(send, keep, other, here, other_b, left_a, left_b, right_a, right_b)
    return finish(place, to_owners(padded, groups), tiles_dev)


def solution(mesh):
    in_specs = (
        P("occ", "vir"),
        P("occ", "vir", None, None),
        P("occ", "vir"),
        P("occ", "vir"),
        P(),
        P(),
    )
    out_specs = P("occ", "vir")
    return jax.shard_map(shards, mesh=mesh, in_specs=in_specs, out_specs=out_specs, check_vma=False)
```

```python
import functools

import jax
import jax.numpy as jnp
from jax import lax
from jax.experimental import pallas as pl
from jax.experimental.pallas import tpu as pltpu
from jax.sharding import PartitionSpec as P

N_Y = 4
N_XH = 2
N_Z = 8
N_XL = 2
ROWS_A = 40
PRODUCT_MIB = 62


def from_occ(v, dx, dy):
    perm = [
        (((a + dx) % N_XH) * N_Y + (b + dy) % N_Y, a * N_Y + b)
        for a in range(N_XH)
        for b in range(N_Y)
    ]
    return lax.ppermute(v, "occ", perm)


def from_vir(v, dx, dc):
    perm = [
        ((((a + dx) % N_XL) * N_Z + z) * 2 + (c + dc) % 2, (a * N_Z + z) * 2 + c)
        for a in range(N_XL)
        for z in range(N_Z)
        for c in range(2)
    ]
    return lax.ppermute(v, "vir", perm)


def smem():
    return pl.BlockSpec(memory_space=pltpu.SMEM)


def vmem():
    return pl.BlockSpec(memory_space=pltpu.VMEM)


def hbm():
    return pl.BlockSpec(memory_space=pltpu.HBM)


def call(kernel, out_shape, in_specs, out_specs, scratch, nbytes, flops=0, limit=8):
    return pl.pallas_call(
        kernel,
        out_shape=out_shape,
        in_specs=in_specs,
        out_specs=out_specs,
        scratch_shapes=scratch,
        compiler_params=pltpu.CompilerParams(vmem_limit_bytes=limit * 1024 * 1024),
        cost_estimate=pl.CostEstimate(flops=flops, bytes_accessed=nbytes, transcendentals=0),
    )


def product_kernel(n_pieces, moves, *refs):
    con_ref, slot_ref, blocks = refs[:3]
    pieces = refs[3 : 3 + n_pieces]
    b_ref, t_ref, x_ref, acc_ref, block_sems, in_sems, out_sems = refs[-7:]
    outs = refs[3 + n_pieces : -7]
    n_blocks, width, _ = b_ref.shape
    n_parts = block_sems.shape[0]
    part = n_blocks // n_parts
    tiles = x_ref.shape[0]
    loads = []
    rows = pieces[0].shape[0]
    for i, piece in enumerate(pieces):
        load = pltpu.make_async_copy(piece, t_ref.at[pl.ds(i * rows, rows)], in_sems.at[i])
        load.start()
        loads.append(load)
    block_loads = []
    for i in range(n_parts):
        some = pl.ds(i * part, part)
        load = pltpu.make_async_copy(blocks.at[some], b_ref.at[some], block_sems.at[i])
        load.start()
        block_loads.append(load)
    acc_ref[...] = jnp.zeros_like(acc_ref)
    for i, load in enumerate(loads):
        load.wait()
        here = slice(i * rows, (i + 1) * rows)
        for c in range(tiles):
            a = t_ref[here, c * width : (c + 1) * width]
            high = a.astype(jnp.bfloat16)
            x_ref[c, here, :width] = high
            x_ref[c, here, width:] = (a - high.astype(jnp.float32)).astype(jnp.bfloat16)
    step = 4

    def body(k, carry):
        results = []
        for u in range(step):
            b = b_ref[k * step + u]
            high = b.astype(jnp.bfloat16)
            low = (b - high.astype(jnp.float32)).astype(jnp.bfloat16)
            w = jnp.concatenate([high, low], axis=1)
            w = jnp.concatenate([w, w], axis=0)
            x = x_ref[con_ref[0, k * step + u]]
            p = jnp.dot(x, w, preferred_element_type=jnp.float32)
            results.append(p[:, :width] + p[:, width:])
        for u in range(step):
            s = slot_ref[0, k * step + u]
            acc_ref[s] = acc_ref[s] + results[u]
        return carry

    for i, load in enumerate(block_loads):
        load.wait()
        lax.fori_loop(i * part // step, (i + 1) * part // step, body, 0)
    stores = []
    for n, (o, index, slot, slots, row, n_rows) in enumerate(moves):
        source = acc_ref.at[pl.ds(slot, slots), pl.ds(row, n_rows)]
        target = outs[o] if index is None else outs[o].at[index]
        store = pltpu.make_async_copy(source, target, out_sems.at[n])
        store.start()
        stores.append(store)
    for store in stores:
        store.wait()


def products(con, slot, blocks, pieces, slots, shapes, moves):
    n_blocks, width, _ = blocks.shape
    tiles = pieces[0].shape[1] // width
    n_rows = pieces[0].shape[0] * len(pieces)
    shapes = [jax.ShapeDtypeStruct(s, jnp.float32) for s in shapes]
    return call(
        functools.partial(product_kernel, len(pieces), moves),
        shapes,
        [smem(), smem()] + [hbm()] * (1 + len(pieces)),
        [hbm()] * len(shapes),
        [
            pltpu.VMEM(blocks.shape, jnp.float32),
            pltpu.VMEM((n_rows, tiles * width), jnp.float32),
            pltpu.VMEM((tiles, n_rows, 2 * width), jnp.bfloat16),
            pltpu.VMEM((slots, n_rows, width), jnp.float32),
            pltpu.SemaphoreType.DMA((4,)),
            pltpu.SemaphoreType.DMA((len(pieces),)),
            pltpu.SemaphoreType.DMA((len(moves),)),
        ],
        4 * (blocks.size + n_rows * (tiles + slots) * width),
        8 * n_blocks * n_rows * width * width,
        PRODUCT_MIB,
    )(con, slot, blocks, *pieces)


def sum_kernel(own, left_a, left_b, right_a, right_b, keep, give):
    half = left_a.shape[1]
    for out, d in ((give, 1), (keep, 0)):
        out[:half] = own[d, :half] + left_a[d] + right_a[d]
        out[half:] = own[d, half:] + left_b[d] + right_b[d]


def y_sum(own, left_a, left_b, right_a, right_b):
    shape = jax.ShapeDtypeStruct(own.shape[1:], jnp.float32)
    return call(sum_kernel, [shape] * 2, [vmem()] * 5, [vmem()] * 2, [], 16 * own.size)(
        own, left_a, left_b, right_a, right_b
    )


def pad_kernel(table, keep, other_a, own, other_b, far, up, down, out, total):
    rows_a = keep.shape[1]
    total[:, :rows_a] = keep[...] + other_a[...]
    total[:, rows_a:] = (own[...] + other_b[3]) + (far[...] + (up[...] + down[...]))

    def body(k, carry):
        s = table[k]
        out[k] = jnp.where(s >= 0, total[jnp.maximum(s, 0)], 0.0)
        return carry

    lax.fori_loop(0, out.shape[0], body, 0, unroll=8)


def pad(table, *terms):
    slots, rows_a, width = terms[0].shape
    rows = rows_a + terms[2].shape[1]
    shape = jax.ShapeDtypeStruct((table.shape[0], rows, width), jnp.float32)
    scratch = [pltpu.VMEM((slots, rows, width), jnp.float32)]
    return call(
        pad_kernel, shape, [smem()] + [vmem()] * 7, vmem(), scratch, 24 * slots * rows * width
    )(table, *terms)


def to_owners(padded, groups):
    n, rows, width = padded.shape
    pieces = lax.all_to_all(padded.reshape(groups, n // groups, rows, width), "vir", 0, 0)
    return pieces.reshape(n, rows, width)


def finish_kernel(place, pieces, out, acc):
    acc[...] = jnp.zeros_like(acc)

    def body(k, carry):
        p = place[k]
        tile = jnp.maximum(p, 0)
        acc[tile] = acc[tile] + jnp.where(p >= 0, pieces[k], 0.0)
        return carry

    lax.fori_loop(0, pieces.shape[0], body, 0, unroll=8)
    tiles, _, width = acc.shape
    for c in range(tiles):
        out[:, c * width : (c + 1) * width] = acc[c]


def finish(place, pieces, tiles):
    _, rows, width = pieces.shape
    shape = jax.ShapeDtypeStruct((rows, tiles * width), jnp.float32)
    scratch = [pltpu.VMEM((tiles, rows, width), jnp.float32)]
    return call(finish_kernel, shape, [smem(), vmem()], vmem(), scratch, 4 * pieces.size)(
        place, pieces
    )


def routes(residual_list, owner_pos, tiles_dev, me):
    groups, slots = residual_list.shape
    total = owner_pos.shape[0]
    tiles = jnp.arange(total, dtype=jnp.int32)
    positions = jnp.sum(
        jnp.where(residual_list[:, :, None] == tiles, owner_pos, 0), axis=2, dtype=jnp.int32
    )
    owners = jnp.arange(groups, dtype=jnp.int32)
    index = jnp.arange(slots, dtype=jnp.int32)
    before = index[None, :] < index[:, None]

    def row(v):
        return jnp.sum(jnp.where(owners[:, None] == v, positions, 0), axis=0, dtype=jnp.int32)

    def pick(mask, value):
        rank = jnp.sum(mask[:, None, :] & before, axis=2, dtype=jnp.int32)
        chosen = mask[:, :, None] & (rank[:, :, None] == jnp.arange(2, dtype=jnp.int32))
        return jnp.max(jnp.where(chosen, value[:, :, None], -1), axis=1).reshape(-1)

    own = row(me)
    to_owner = (own // tiles_dev)[None, :] == owners[:, None]
    send = pick(to_owner, jnp.broadcast_to(index, (groups, slots)))
    place = pick(positions // tiles_dev == me, positions % tiles_dev)
    return send, place


def shards(t2, integral_tiles, contract_tile, slot_of_block, residual_list, owner_pos):
    width = integral_tiles.shape[-1]
    tiles_dev = t2.shape[1] // width
    groups, slots = residual_list.shape
    half = slots // 2
    rows_a = ROWS_A
    rows = t2.shape[0]
    rows_b = rows - rows_a

    me = lax.axis_index("vir")
    send, place = routes(residual_list, owner_pos, tiles_dev, me)
    offsets = [(dx, dy) for dy in (2, 1, -1, 0) for dx in (0, 1)]
    pieces = [from_occ(t2, dx, dy) if dx or dy else t2 for dx, dy in offsets]

    one = (slots, rows_b, width)
    shapes = [(2, half, rows_a, width)] * 6 + [(2, slots, rows_a, width)] + [one] * 4 + [(4,) + one]
    moves = []
    for g in range(4):
        for part in range(2) if g < 3 else (None,):
            for d in range(2):
                row = (2 * g + d) * rows
                if part is None:
                    moves.append((6, d, 0, slots, row, rows_a))
                else:
                    moves.append((2 * g + part, d, part * half, half, row, rows_a))
        moves.append((7 + g, None, 0, slots, 2 * g * rows + rows_a, rows_b))
        moves.append((11, g, 0, slots, (2 * g + 1) * rows + rows_a, rows_b))
    far_a, far_b, up_a, up_b, down_a, down_b, own, far, up, down, here, give_b = products(
        contract_tile, slot_of_block, integral_tiles[0], pieces, slots, shapes, moves
    )
    other_b = from_occ(give_b, 1, 0)
    left_far = from_occ(far_a, 0, -1)
    right_far = from_occ(far_b, 0, 1)
    left_b = from_occ(up_b, 0, -1)
    right_a = from_occ(down_a, 0, 1)
    left_a = from_occ(up_a + left_far, 0, -1)
    right_b = from_occ(down_b + right_far, 0, 1)
    sums_a = (own, left_a, left_b, right_a, right_b)

    from_far = from_occ(far + other_b[0], 0, 2)
    from_down = from_occ(up + other_b[1], 0, -1)
    from_up = from_occ(down + other_b[2], 0, 1)

    keep, give = y_sum(*sums_a)
    other = from_occ(give, 1, 0)
    padded = pad(send, keep, other, here, other_b, from_far, from_down, from_up)
    return finish(place, to_owners(padded, groups), tiles_dev)


def solution(mesh):
    in_specs = (
        P("occ", "vir"),
        P("occ", "vir", None, None),
        P("occ", "vir"),
        P("occ", "vir"),
        P(),
        P(),
    )
    out_specs = P("occ", "vir")
    return jax.shard_map(shards, mesh=mesh, in_specs=in_specs, out_specs=out_specs, check_vma=False)
```

```python
import functools

import jax
import jax.numpy as jnp
from jax import lax
from jax.experimental import pallas as pl
from jax.experimental.pallas import tpu as pltpu
from jax.sharding import PartitionSpec as P

N_Y = 4
N_XH = 2
N_Z = 8
N_XL = 2
ROWS_A = 40
PRODUCT_MIB = 62


def from_occ(v, dx, dy):
    perm = [
        (((a + dx) % N_XH) * N_Y + (b + dy) % N_Y, a * N_Y + b)
        for a in range(N_XH)
        for b in range(N_Y)
    ]
    return lax.ppermute(v, "occ", perm)


def from_vir(v, dx, dc):
    perm = [
        ((((a + dx) % N_XL) * N_Z + z) * 2 + (c + dc) % 2, (a * N_Z + z) * 2 + c)
        for a in range(N_XL)
        for z in range(N_Z)
        for c in range(2)
    ]
    return lax.ppermute(v, "vir", perm)


def smem():
    return pl.BlockSpec(memory_space=pltpu.SMEM)


def vmem():
    return pl.BlockSpec(memory_space=pltpu.VMEM)


def hbm():
    return pl.BlockSpec(memory_space=pltpu.HBM)


def call(kernel, out_shape, in_specs, out_specs, scratch, nbytes, flops=0, limit=8):
    return pl.pallas_call(
        kernel,
        out_shape=out_shape,
        in_specs=in_specs,
        out_specs=out_specs,
        scratch_shapes=scratch,
        compiler_params=pltpu.CompilerParams(vmem_limit_bytes=limit * 1024 * 1024),
        cost_estimate=pl.CostEstimate(flops=flops, bytes_accessed=nbytes, transcendentals=0),
    )


def product_kernel(n_pieces, moves, *refs):
    con_ref, slot_ref, blocks = refs[:3]
    pieces = refs[3 : 3 + n_pieces]
    b_ref, t_ref, x_ref, acc_ref, block_sems, in_sems, out_sems = refs[-7:]
    outs = refs[3 + n_pieces : -7]
    n_blocks, width, _ = b_ref.shape
    n_parts = block_sems.shape[0]
    part = n_blocks // n_parts
    tiles = x_ref.shape[0]
    loads = []
    rows = pieces[0].shape[0]
    for i, piece in enumerate(pieces):
        load = pltpu.make_async_copy(piece, t_ref.at[pl.ds(i * rows, rows)], in_sems.at[i])
        load.start()
        loads.append(load)
    block_loads = []
    for i in range(n_parts):
        some = pl.ds(i * part, part)
        load = pltpu.make_async_copy(blocks.at[some], b_ref.at[some], block_sems.at[i])
        load.start()
        block_loads.append(load)
    acc_ref[...] = jnp.zeros_like(acc_ref)
    for i, load in enumerate(loads):
        load.wait()
        here = slice(i * rows, (i + 1) * rows)
        for c in range(tiles):
            a = t_ref[here, c * width : (c + 1) * width]
            high = a.astype(jnp.bfloat16)
            x_ref[c, here, :width] = high
            x_ref[c, here, width:] = (a - high.astype(jnp.float32)).astype(jnp.bfloat16)
    step = 8

    def body(k, carry):
        results = []
        for u in range(step):
            b = b_ref[k * step + u]
            high = b.astype(jnp.bfloat16)
            low = (b - high.astype(jnp.float32)).astype(jnp.bfloat16)
            w = jnp.concatenate([high, low], axis=1)
            w = jnp.concatenate([w, w], axis=0)
            x = x_ref[con_ref[0, k * step + u]]
            p = jnp.dot(x, w, preferred_element_type=jnp.float32)
            results.append(p[:, :width] + p[:, width:])
        for u in range(step):
            s = slot_ref[0, k * step + u]
            acc_ref[s] = acc_ref[s] + results[u]
        return carry

    for i, load in enumerate(block_loads):
        load.wait()
        lax.fori_loop(i * part // step, (i + 1) * part // step, body, 0)
    stores = []
    for n, (o, index, slot, slots, row, n_rows) in enumerate(moves):
        source = acc_ref.at[pl.ds(slot, slots), pl.ds(row, n_rows)]
        target = outs[o] if index is None else outs[o].at[index]
        store = pltpu.make_async_copy(source, target, out_sems.at[n])
        store.start()
        stores.append(store)
    for store in stores:
        store.wait()


def products(con, slot, blocks, pieces, slots, shapes, moves):
    n_blocks, width, _ = blocks.shape
    tiles = pieces[0].shape[1] // width
    n_rows = pieces[0].shape[0] * len(pieces)
    shapes = [jax.ShapeDtypeStruct(s, jnp.float32) for s in shapes]
    return call(
        functools.partial(product_kernel, len(pieces), moves),
        shapes,
        [smem(), smem()] + [hbm()] * (1 + len(pieces)),
        [hbm()] * len(shapes),
        [
            pltpu.VMEM(blocks.shape, jnp.float32),
            pltpu.VMEM((n_rows, tiles * width), jnp.float32),
            pltpu.VMEM((tiles, n_rows, 2 * width), jnp.bfloat16),
            pltpu.VMEM((slots, n_rows, width), jnp.float32),
            pltpu.SemaphoreType.DMA((4,)),
            pltpu.SemaphoreType.DMA((len(pieces),)),
            pltpu.SemaphoreType.DMA((len(moves),)),
        ],
        4 * (blocks.size + n_rows * (tiles + slots) * width),
        8 * n_blocks * n_rows * width * width,
        PRODUCT_MIB,
    )(con, slot, blocks, *pieces)


def sum_kernel(own, left_a, left_b, right_a, right_b, keep, give):
    half = left_a.shape[1]
    for out, d in ((give, 1), (keep, 0)):
        out[:half] = own[d, :half] + left_a[d] + right_a[d]
        out[half:] = own[d, half:] + left_b[d] + right_b[d]


def y_sum(own, left_a, left_b, right_a, right_b):
    shape = jax.ShapeDtypeStruct(own.shape[1:], jnp.float32)
    return call(sum_kernel, [shape] * 2, [vmem()] * 5, [vmem()] * 2, [], 16 * own.size)(
        own, left_a, left_b, right_a, right_b
    )


def pad_kernel(table, keep, other_a, own, other_b, far, up, down, out, total):
    rows_a = keep.shape[1]
    total[:, :rows_a] = keep[...] + other_a[...]
    total[:, rows_a:] = (own[...] + other_b[3]) + (far[...] + (up[...] + down[...]))

    def body(k, carry):
        s = table[k]
        out[k] = jnp.where(s >= 0, total[jnp.maximum(s, 0)], 0.0)
        return carry

    lax.fori_loop(0, out.shape[0], body, 0, unroll=8)


def pad(table, *terms):
    slots, rows_a, width = terms[0].shape
    rows = rows_a + terms[2].shape[1]
    shape = jax.ShapeDtypeStruct((table.shape[0], rows, width), jnp.float32)
    scratch = [pltpu.VMEM((slots, rows, width), jnp.float32)]
    return call(
        pad_kernel, shape, [smem()] + [vmem()] * 7, vmem(), scratch, 24 * slots * rows * width
    )(table, *terms)


def to_owners(padded, groups):
    n, rows, width = padded.shape
    pieces = lax.all_to_all(padded.reshape(groups, n // groups, rows, width), "vir", 0, 0)
    return pieces.reshape(n, rows, width)


def finish_kernel(place, pieces, out, acc):
    acc[...] = jnp.zeros_like(acc)

    def body(k, carry):
        p = place[k]
        tile = jnp.maximum(p, 0)
        acc[tile] = acc[tile] + jnp.where(p >= 0, pieces[k], 0.0)
        return carry

    lax.fori_loop(0, pieces.shape[0], body, 0, unroll=8)
    tiles, _, width = acc.shape
    for c in range(tiles):
        out[:, c * width : (c + 1) * width] = acc[c]


def finish(place, pieces, tiles):
    _, rows, width = pieces.shape
    shape = jax.ShapeDtypeStruct((rows, tiles * width), jnp.float32)
    scratch = [pltpu.VMEM((tiles, rows, width), jnp.float32)]
    return call(finish_kernel, shape, [smem(), vmem()], vmem(), scratch, 4 * pieces.size)(
        place, pieces
    )


def routes(residual_list, owner_pos, tiles_dev, me):
    groups, slots = residual_list.shape
    total = owner_pos.shape[0]
    tiles = jnp.arange(total, dtype=jnp.int32)
    positions = jnp.sum(
        jnp.where(residual_list[:, :, None] == tiles, owner_pos, 0), axis=2, dtype=jnp.int32
    )
    owners = jnp.arange(groups, dtype=jnp.int32)
    index = jnp.arange(slots, dtype=jnp.int32)
    before = index[None, :] < index[:, None]

    def row(v):
        return jnp.sum(jnp.where(owners[:, None] == v, positions, 0), axis=0, dtype=jnp.int32)

    def pick(mask, value):
        rank = jnp.sum(mask[:, None, :] & before, axis=2, dtype=jnp.int32)
        chosen = mask[:, :, None] & (rank[:, :, None] == jnp.arange(2, dtype=jnp.int32))
        return jnp.max(jnp.where(chosen, value[:, :, None], -1), axis=1).reshape(-1)

    own = row(me)
    to_owner = (own // tiles_dev)[None, :] == owners[:, None]
    send = pick(to_owner, jnp.broadcast_to(index, (groups, slots)))
    place = pick(positions // tiles_dev == me, positions % tiles_dev)
    return send, place


def shards(t2, integral_tiles, contract_tile, slot_of_block, residual_list, owner_pos):
    width = integral_tiles.shape[-1]
    tiles_dev = t2.shape[1] // width
    groups, slots = residual_list.shape
    half = slots // 2
    rows_a = ROWS_A
    rows = t2.shape[0]
    rows_b = rows - rows_a

    me = lax.axis_index("vir")
    send, place = routes(residual_list, owner_pos, tiles_dev, me)
    offsets = [(dx, dy) for dy in (2, 1, -1, 0) for dx in (0, 1)]
    pieces = [from_occ(t2, dx, dy) if dx or dy else t2 for dx, dy in offsets]

    one = (slots, rows_b, width)
    shapes = [(2, half, rows_a, width)] * 6 + [(2, slots, rows_a, width)] + [one] * 4 + [(4,) + one]
    moves = []
    for g in range(4):
        for part in range(2) if g < 3 else (None,):
            for d in range(2):
                row = (2 * g + d) * rows
                if part is None:
                    moves.append((6, d, 0, slots, row, rows_a))
                else:
                    moves.append((2 * g + part, d, part * half, half, row, rows_a))
        moves.append((7 + g, None, 0, slots, 2 * g * rows + rows_a, rows_b))
        moves.append((11, g, 0, slots, (2 * g + 1) * rows + rows_a, rows_b))
    far_a, far_b, up_a, up_b, down_a, down_b, own, far, up, down, here, give_b = products(
        contract_tile, slot_of_block, integral_tiles[0], pieces, slots, shapes, moves
    )
    other_b = from_occ(give_b, 1, 0)
    left_far = from_occ(far_a, 0, -1)
    right_far = from_occ(far_b, 0, 1)
    left_b = from_occ(up_b, 0, -1)
    right_a = from_occ(down_a, 0, 1)
    left_a = from_occ(up_a + left_far, 0, -1)
    right_b = from_occ(down_b + right_far, 0, 1)
    sums_a = (own, left_a, left_b, right_a, right_b)

    from_far = from_occ(far + other_b[0], 0, 2)
    from_down = from_occ(up + other_b[1], 0, -1)
    from_up = from_occ(down + other_b[2], 0, 1)

    keep, give = y_sum(*sums_a)
    other = from_occ(give, 1, 0)
    padded = pad(send, keep, other, here, other_b, from_far, from_down, from_up)
    return finish(place, to_owners(padded, groups), tiles_dev)


def solution(mesh):
    in_specs = (
        P("occ", "vir"),
        P("occ", "vir", None, None),
        P("occ", "vir"),
        P("occ", "vir"),
        P(),
        P(),
    )
    out_specs = P("occ", "vir")
    return jax.shard_map(shards, mesh=mesh, in_specs=in_specs, out_specs=out_specs, check_vma=False)
```

```python
import functools

import jax
import jax.numpy as jnp
from jax import lax
from jax.experimental import pallas as pl
from jax.experimental.pallas import tpu as pltpu
from jax.sharding import PartitionSpec as P

N_Y = 4
N_XH = 2
N_Z = 8
N_XL = 2
ROWS_A = 40
PRODUCT_MIB = 62


def from_occ(v, dx, dy):
    perm = [
        (((a + dx) % N_XH) * N_Y + (b + dy) % N_Y, a * N_Y + b)
        for a in range(N_XH)
        for b in range(N_Y)
    ]
    return lax.ppermute(v, "occ", perm)


def from_vir(v, dx, dc):
    perm = [
        ((((a + dx) % N_XL) * N_Z + z) * 2 + (c + dc) % 2, (a * N_Z + z) * 2 + c)
        for a in range(N_XL)
        for z in range(N_Z)
        for c in range(2)
    ]
    return lax.ppermute(v, "vir", perm)


def smem():
    return pl.BlockSpec(memory_space=pltpu.SMEM)


def vmem():
    return pl.BlockSpec(memory_space=pltpu.VMEM)


def hbm():
    return pl.BlockSpec(memory_space=pltpu.HBM)


def call(kernel, out_shape, in_specs, out_specs, scratch, nbytes, flops=0, limit=8):
    return pl.pallas_call(
        kernel,
        out_shape=out_shape,
        in_specs=in_specs,
        out_specs=out_specs,
        scratch_shapes=scratch,
        compiler_params=pltpu.CompilerParams(vmem_limit_bytes=limit * 1024 * 1024),
        cost_estimate=pl.CostEstimate(flops=flops, bytes_accessed=nbytes, transcendentals=0),
    )


def product_kernel(n_pieces, moves, *refs):
    con_ref, slot_ref, blocks = refs[:3]
    pieces = refs[3 : 3 + n_pieces]
    b_ref, t_ref, x_ref, acc_ref, block_sems, in_sems, out_sems = refs[-7:]
    outs = refs[3 + n_pieces : -7]
    n_blocks, width, _ = b_ref.shape
    n_parts = block_sems.shape[0]
    part = n_blocks // n_parts
    tiles = x_ref.shape[0]
    loads = []
    rows = pieces[0].shape[0]
    for i, piece in enumerate(pieces):
        load = pltpu.make_async_copy(piece, t_ref.at[pl.ds(i * rows, rows)], in_sems.at[i])
        load.start()
        loads.append(load)
    block_loads = []
    for i in range(n_parts):
        some = pl.ds(i * part, part)
        load = pltpu.make_async_copy(blocks.at[some], b_ref.at[some], block_sems.at[i])
        load.start()
        block_loads.append(load)
    acc_ref[...] = jnp.zeros_like(acc_ref)
    for i, load in enumerate(loads):
        load.wait()
        here = slice(i * rows, (i + 1) * rows)
        for c in range(tiles):
            a = t_ref[here, c * width : (c + 1) * width]
            high = a.astype(jnp.bfloat16)
            x_ref[c, here, :width] = high
            x_ref[c, here, width:] = (a - high.astype(jnp.float32)).astype(jnp.bfloat16)
    step = 16

    def body(k, carry):
        results = []
        for u in range(step):
            b = b_ref[k * step + u]
            high = b.astype(jnp.bfloat16)
            low = (b - high.astype(jnp.float32)).astype(jnp.bfloat16)
            w = jnp.concatenate([high, low], axis=1)
            w = jnp.concatenate([w, w], axis=0)
            x = x_ref[con_ref[0, k * step + u]]
            p = jnp.dot(x, w, preferred_element_type=jnp.float32)
            results.append(p[:, :width] + p[:, width:])
        for u in range(step):
            s = slot_ref[0, k * step + u]
            acc_ref[s] = acc_ref[s] + results[u]
        return carry

    for i, load in enumerate(block_loads):
        load.wait()
        lax.fori_loop(i * part // step, (i + 1) * part // step, body, 0)
    stores = []
    for n, (o, index, slot, slots, row, n_rows) in enumerate(moves):
        source = acc_ref.at[pl.ds(slot, slots), pl.ds(row, n_rows)]
        target = outs[o] if index is None else outs[o].at[index]
        store = pltpu.make_async_copy(source, target, out_sems.at[n])
        store.start()
        stores.append(store)
    for store in stores:
        store.wait()


def products(con, slot, blocks, pieces, slots, shapes, moves):
    n_blocks, width, _ = blocks.shape
    tiles = pieces[0].shape[1] // width
    n_rows = pieces[0].shape[0] * len(pieces)
    shapes = [jax.ShapeDtypeStruct(s, jnp.float32) for s in shapes]
    return call(
        functools.partial(product_kernel, len(pieces), moves),
        shapes,
        [smem(), smem()] + [hbm()] * (1 + len(pieces)),
        [hbm()] * len(shapes),
        [
            pltpu.VMEM(blocks.shape, jnp.float32),
            pltpu.VMEM((n_rows, tiles * width), jnp.float32),
            pltpu.VMEM((tiles, n_rows, 2 * width), jnp.bfloat16),
            pltpu.VMEM((slots, n_rows, width), jnp.float32),
            pltpu.SemaphoreType.DMA((4,)),
            pltpu.SemaphoreType.DMA((len(pieces),)),
            pltpu.SemaphoreType.DMA((len(moves),)),
        ],
        4 * (blocks.size + n_rows * (tiles + slots) * width),
        8 * n_blocks * n_rows * width * width,
        PRODUCT_MIB,
    )(con, slot, blocks, *pieces)


def sum_kernel(own, left_a, left_b, right_a, right_b, keep, give):
    half = left_a.shape[1]
    for out, d in ((give, 1), (keep, 0)):
        out[:half] = own[d, :half] + left_a[d] + right_a[d]
        out[half:] = own[d, half:] + left_b[d] + right_b[d]


def y_sum(own, left_a, left_b, right_a, right_b):
    shape = jax.ShapeDtypeStruct(own.shape[1:], jnp.float32)
    return call(sum_kernel, [shape] * 2, [vmem()] * 5, [vmem()] * 2, [], 16 * own.size)(
        own, left_a, left_b, right_a, right_b
    )


def pad_kernel(table, keep, other_a, own, other_b, far, up, down, out, total):
    rows_a = keep.shape[1]
    total[:, :rows_a] = keep[...] + other_a[...]
    total[:, rows_a:] = (own[...] + other_b[3]) + (far[...] + (up[...] + down[...]))

    def body(k, carry):
        s = table[k]
        out[k] = jnp.where(s >= 0, total[jnp.maximum(s, 0)], 0.0)
        return carry

    lax.fori_loop(0, out.shape[0], body, 0, unroll=8)


def pad(table, *terms):
    slots, rows_a, width = terms[0].shape
    rows = rows_a + terms[2].shape[1]
    shape = jax.ShapeDtypeStruct((table.shape[0], rows, width), jnp.float32)
    scratch = [pltpu.VMEM((slots, rows, width), jnp.float32)]
    return call(
        pad_kernel, shape, [smem()] + [vmem()] * 7, vmem(), scratch, 24 * slots * rows * width
    )(table, *terms)


def to_owners(padded, groups):
    n, rows, width = padded.shape
    pieces = lax.all_to_all(padded.reshape(groups, n // groups, rows, width), "vir", 0, 0)
    return pieces.reshape(n, rows, width)


def finish_kernel(place, pieces, out, acc):
    acc[...] = jnp.zeros_like(acc)

    def body(k, carry):
        p = place[k]
        tile = jnp.maximum(p, 0)
        acc[tile] = acc[tile] + jnp.where(p >= 0, pieces[k], 0.0)
        return carry

    lax.fori_loop(0, pieces.shape[0], body, 0, unroll=8)
    tiles, _, width = acc.shape
    for c in range(tiles):
        out[:, c * width : (c + 1) * width] = acc[c]


def finish(place, pieces, tiles):
    _, rows, width = pieces.shape
    shape = jax.ShapeDtypeStruct((rows, tiles * width), jnp.float32)
    scratch = [pltpu.VMEM((tiles, rows, width), jnp.float32)]
    return call(finish_kernel, shape, [smem(), vmem()], vmem(), scratch, 4 * pieces.size)(
        place, pieces
    )


def routes(residual_list, owner_pos, tiles_dev, me):
    groups, slots = residual_list.shape
    total = owner_pos.shape[0]
    tiles = jnp.arange(total, dtype=jnp.int32)
    positions = jnp.sum(
        jnp.where(residual_list[:, :, None] == tiles, owner_pos, 0), axis=2, dtype=jnp.int32
    )
    owners = jnp.arange(groups, dtype=jnp.int32)
    index = jnp.arange(slots, dtype=jnp.int32)
    before = index[None, :] < index[:, None]

    def row(v):
        return jnp.sum(jnp.where(owners[:, None] == v, positions, 0), axis=0, dtype=jnp.int32)

    def pick(mask, value):
        rank = jnp.sum(mask[:, None, :] & before, axis=2, dtype=jnp.int32)
        chosen = mask[:, :, None] & (rank[:, :, None] == jnp.arange(2, dtype=jnp.int32))
        return jnp.max(jnp.where(chosen, value[:, :, None], -1), axis=1).reshape(-1)

    own = row(me)
    to_owner = (own // tiles_dev)[None, :] == owners[:, None]
    send = pick(to_owner, jnp.broadcast_to(index, (groups, slots)))
    place = pick(positions // tiles_dev == me, positions % tiles_dev)
    return send, place


def shards(t2, integral_tiles, contract_tile, slot_of_block, residual_list, owner_pos):
    width = integral_tiles.shape[-1]
    tiles_dev = t2.shape[1] // width
    groups, slots = residual_list.shape
    half = slots // 2
    rows_a = ROWS_A
    rows = t2.shape[0]
    rows_b = rows - rows_a

    me = lax.axis_index("vir")
    send, place = routes(residual_list, owner_pos, tiles_dev, me)
    offsets = [(dx, dy) for dy in (2, 1, -1, 0) for dx in (0, 1)]
    pieces = [from_occ(t2, dx, dy) if dx or dy else t2 for dx, dy in offsets]

    one = (slots, rows_b, width)
    shapes = [(2, half, rows_a, width)] * 6 + [(2, slots, rows_a, width)] + [one] * 4 + [(4,) + one]
    moves = []
    for g in range(4):
        for part in range(2) if g < 3 else (None,):
            for d in range(2):
                row = (2 * g + d) * rows
                if part is None:
                    moves.append((6, d, 0, slots, row, rows_a))
                else:
                    moves.append((2 * g + part, d, part * half, half, row, rows_a))
        moves.append((7 + g, None, 0, slots, 2 * g * rows + rows_a, rows_b))
        moves.append((11, g, 0, slots, (2 * g + 1) * rows + rows_a, rows_b))
    far_a, far_b, up_a, up_b, down_a, down_b, own, far, up, down, here, give_b = products(
        contract_tile, slot_of_block, integral_tiles[0], pieces, slots, shapes, moves
    )
    other_b = from_occ(give_b, 1, 0)
    left_far = from_occ(far_a, 0, -1)
    right_far = from_occ(far_b, 0, 1)
    left_b = from_occ(up_b, 0, -1)
    right_a = from_occ(down_a, 0, 1)
    left_a = from_occ(up_a + left_far, 0, -1)
    right_b = from_occ(down_b + right_far, 0, 1)
    sums_a = (own, left_a, left_b, right_a, right_b)

    from_far = from_occ(far + other_b[0], 0, 2)
    from_down = from_occ(up + other_b[1], 0, -1)
    from_up = from_occ(down + other_b[2], 0, 1)

    keep, give = y_sum(*sums_a)
    other = from_occ(give, 1, 0)
    padded = pad(send, keep, other, here, other_b, from_far, from_down, from_up)
    return finish(place, to_owners(padded, groups), tiles_dev)


def solution(mesh):
    in_specs = (
        P("occ", "vir"),
        P("occ", "vir", None, None),
        P("occ", "vir"),
        P("occ", "vir"),
        P(),
        P(),
    )
    out_specs = P("occ", "vir")
    return jax.shard_map(shards, mesh=mesh, in_specs=in_specs, out_specs=out_specs, check_vma=False)
```
